256 devices in a mesh: leaf: 128 (over y, z, x), col: 2 (over core).
Axes of the slice: x: 4, y: 4, z: 8, core: 2. Of those that a mesh axis runs over, the one named last changes fastest.
Arguments:
- near_tiles: bfloat16 [1024, 9, 256, 256], P('leaf'), may hold values from -0.125 to 0.125
- block_cols: int32 [1024, 9], P('leaf'), may hold values from 0 to 1023, as said below
- row_counts: int32 [1024], P('leaf'), may hold values from 3 to 9
- random_cols: bfloat16 [1024, 256, 256], P('leaf', None, 'col'), may hold values from -6 to 6
Outputs:
- leaf_basis: float32 [512, 512, 256], P('leaf', None, 'col')
- inner_transfer: float32 [384, 512, 256], P('leaf', None, 'col')
- upper_transfer: float32 [128, 4, 256, 256], P('leaf', None, None, 'col')
The draws below stay inside these ranges and needn't reach their ends.
Inputs may be any that keep to these rules, and one draw needn't show every extreme that they name: `block_cols`: slot 0 of block row r is r itself; every block column lies within 8 blocks of its block row.
All inputs are finite; a program needn't handle non-finite values.
Results may differ from the reference program's by a relative error of at most 0.0003.
Values may be sent and summed in bfloat16 or wider, within the bound.
No kernel may reach another device: no remote copies, remote signals or barrier semaphores. Data moves between devices by JAX's collectives and lax.ppermute only.
A program may use at most 128 MiB of HBM per device.

```python
import math
import jax
import jax.numpy as jnp
import numpy as np
from jax import lax

TILE = 256
SAMPLES = 256
NNZ = 9
LPD = 4
UP = 4
BPD = 8
NB = 1024
NLEAVES = 512
N_LEAF = 128


def draw_block_cols(key, part):
    key = jax.random.fold_in(key, 11)
    row_ids = jnp.arange(NB, dtype=jnp.int32)[:, None]
    offsets = jax.random.randint(key, (NB, NNZ), -BPD, BPD + 1, dtype=jnp.int32)
    offsets = offsets.at[:, 0].set(0)
    return jnp.clip(row_ids + offsets, 0, NB - 1).astype(jnp.int32)


def draw_row_counts(key, part):
    key = jax.random.fold_in(key, 23)
    counts = jax.random.randint(key, (NB,), 3, NNZ + 1, dtype=jnp.int32)
    return counts.at[0].set(NNZ).at[1].set(3)


def steps_of(own_key, dims, shards, low, largest):
    factor_of, own = 1.0, jax.random.fold_in(own_key, 6)
    for dim, shards_of in shards:
        steps = jnp.exp(jax.random.uniform(jax.random.fold_in(own, dim), (shards_of,), jnp.float32, low / len(shards), largest / len(shards)))
        factor_of = factor_of * jnp.repeat(steps, dims[dim] // shards_of).reshape([-1 if axis == dim else 1 for axis in range(len(dims))])
    return factor_of


def gaussian(rng, shape, spread, reach, cuts=(), kind=jnp.bfloat16):
    array = spread * jax.random.normal(rng, shape, jnp.float32)
    if cuts:
        array = array * steps_of(rng, shape, cuts, -0.22, 0.18)
    return jnp.clip(array, -reach, reach).astype(kind)


def setup_inputs(seed: int = 0) -> dict:
    streams_of = jax.random.split(jax.random.key(seed), 5)
    near_tiles = gaussian(streams_of[0], (NB, NNZ, TILE, TILE), (TILE * NNZ) ** -0.5, 0.125, ((0, 128),))
    block_cols = draw_block_cols(jax.random.fold_in(streams_of[4], 71), 0)
    row_counts = draw_row_counts(jax.random.fold_in(streams_of[4], 71), 0)
    random_cols = gaussian(streams_of[3], (NB, TILE, SAMPLES), 1.0, 6.0, ((0, 128), (2, 2)))
    return {"near_tiles": near_tiles, "block_cols": block_cols, "row_counts": row_counts, "random_cols": random_cols}


def right_solve(chol_all, right_rows):
    return lax.linalg.triangular_solve(chol_all, right_rows, left_side=False, lower=True, transpose_a=True)

def gram_of(block_rows):
    return jnp.einsum('nrs,nrt->nst', block_rows, block_rows, precision=lax.Precision.HIGHEST)

def reference(near_tiles, block_cols, row_counts, random_cols):
    slot_ids = jnp.arange(NNZ, dtype=jnp.int32)

    def one_row(items):
        tile_row, col_row, count_row = items
        slabs = random_cols[col_row]
        keep_slot = slot_ids < count_row
        slabs = jnp.where(keep_slot[:, None, None], slabs, jnp.zeros_like(slabs))
        flat_tiles = jnp.transpose(tile_row, (1, 0, 2)).reshape(TILE, NNZ * TILE)
        return jnp.dot(flat_tiles.astype(jnp.float32), slabs.reshape(NNZ * TILE, SAMPLES).astype(jnp.float32), preferred_element_type=jnp.float32)
    samples = lax.map(one_row, (near_tiles, block_cols, row_counts))
    leaf_samples = samples.reshape(NLEAVES, 2 * TILE, SAMPLES)
    gram_now = gram_of(leaf_samples)
    chol_now = jnp.linalg.cholesky(gram_now)
    leaf_basis = right_solve(chol_now, leaf_samples) * math.sqrt(2 * TILE)
    scale_pair = math.sqrt(2 * SAMPLES)
    pieces = []
    for level_id in range(LPD.bit_length() - 1):
        gram_par = gram_now[0::2] + gram_now[1::2]
        chol_par = jnp.linalg.cholesky(gram_par)
        stacked = jnp.concatenate([jnp.transpose(chol_now[0::2], (0, 2, 1)), jnp.transpose(chol_now[1::2], (0, 2, 1))], axis=1)
        transfer = right_solve(chol_par, stacked) * scale_pair
        pieces.append(transfer.reshape(N_LEAF, -1, 2 * SAMPLES, SAMPLES))
        gram_now, chol_now = (gram_par, chol_par)
    inner_transfer = jnp.concatenate(pieces, axis=1).reshape(N_LEAF * (LPD - 1), 2 * SAMPLES, SAMPLES)
    uppers = []
    for level_id in range(UP):
        partner = np.arange(N_LEAF) ^ 1 << level_id
        gram_par = gram_now + gram_now[partner]
        chol_par = jnp.linalg.cholesky(gram_par)
        uppers.append(right_solve(chol_par, jnp.transpose(chol_now, (0, 2, 1))) * scale_pair)
        gram_now, chol_now = (gram_par, chol_par)
    upper_transfer = jnp.stack(uppers, axis=1)
    return (leaf_basis, inner_transfer, upper_transfer)
```

```python
import math

import jax
import jax.numpy as jnp
from jax import lax
from jax.experimental import pallas as pl
from jax.experimental.pallas import tpu as pltpu
from jax.sharding import PartitionSpec as P

N = 256
UP = 4
NB = 64

def halves(x):
    high = x.astype(jnp.bfloat16)
    low = (x - high.astype(jnp.float32)).astype(jnp.bfloat16)
    return high, low

def dot(a, b, dims):
    return lax.dot_general(a, b, (dims, ((), ())), preferred_element_type=jnp.float32)

def dot3(a, b, dims):
    ah, al = halves(a)
    bh, bl = halves(b)
    return dot(ah, bh, dims) + (dot(ah, bl, dims) + dot(al, bh, dims))

NN = ((1,), (0,))
NT = ((1,), (1,))
TN = ((0,), (0,))

def factor(x_ref, m_ref, r_ref):
    batch = x_ref.shape[0]
    sub = lax.broadcasted_iota(jnp.int32, (1, 8, 128), 1)
    lane64 = lax.broadcasted_iota(jnp.int32, (NB, 128), 1)
    row64 = lax.broadcasted_iota(jnp.int32, (NB, 128), 0)
    lane8 = lax.broadcasted_iota(jnp.int32, (1, 8, 128), 2)
    full = (batch, 8, 128)
    for p in range(N // NB):
        o = p * NB
        base = o % 128
        other = NB - base
        c0 = o - base
        in_d = (lane64 >= base) & (lane64 < base + NB)
        eye = jnp.where(lane64 - other == row64, 1.0, 0.0).astype(jnp.float32)
        for b in range(batch):
            m_ref[b] = jnp.where(in_d, x_ref[b, o:o + NB, c0:c0 + 128], eye)
        for g in range(NB // 8):
            k0 = base + 8 * g
            top = m_ref[:, 8 * g:8 * g + 8, :]
            cols = [jnp.broadcast_to(top[:, :, k0 + j:k0 + j + 1], full) for j in range(8)]
            t = top
            w = top
            rd_all = jnp.ones(full, jnp.float32)
            trows = []
            for j in range(8):
                rd = jnp.broadcast_to((1.0 / cols[j])[:, j:j + 1, :], full)
                f = jnp.where(sub == j, 0.0, cols[j] * rd)
                trow = jnp.broadcast_to(t[:, j:j + 1, :], full)
                w = jnp.where(sub == j, trow, w)
                rd_all = jnp.where(sub == j, rd, rd_all)
                t = t - f * trow
                for jj in range(j + 1, 8):
                    cols[jj] = cols[jj] - f * jnp.broadcast_to(cols[jj][:, j:j + 1, :], full)
            t = t * rd_all
            w = w * jnp.sqrt(rd_all)
            m_ref[:, 8 * g:8 * g + 8, :] = w
            if g < NB // 8 - 1:
                trows = [jnp.broadcast_to(t[:, j:j + 1, :], full) for j in range(8)]
                for h in range(g + 1, NB // 8):
                    low = m_ref[:, 8 * h:8 * h + 8, :]
                    acc = low
                    for j in range(8):
                        acc = acc - jnp.broadcast_to(low[:, :, k0 + j:k0 + j + 1], full) * trows[j]
                    m_ref[:, 8 * h:8 * h + 8, :] = acc
        for b in range(batch):
            m = m_ref[b]
            inv = m[:, other:other + NB]
            spun = pltpu.roll(m, NB, 1)
            row = dot3(inv, x_ref[b, o:o + NB, :], NN)
            mid = jnp.where(in_d, spun, row[:, c0:c0 + 128])
            row = jnp.concatenate([mid, row[:, 128:]] if c0 == 0 else [row[:, :128], mid], axis=1)
            diag = jnp.where(in_d & (lane64 - base >= row64), m, 0.0)
            if base == 0:
                diag = jnp.where(in_d, diag, row[:, c0:c0 + 128])
            if c0 == 0:
                r_ref[b, o:o + NB, 0:128] = diag
                r_ref[b, o:o + NB, 128:256] = row[:, 128:256]
            else:
                r_ref[b, o:o + NB, 0:128] = jnp.zeros((NB, 128), jnp.float32)
                r_ref[b, o:o + NB, 128:256] = diag
            if c0 == 0:
                keep = jnp.where(lane64 < base + NB, row[:, 0:128], 0.0)
                x_ref[b, o:o + NB, 0:128] = keep
                x_ref[b, o:o + NB, 128:256] = jnp.zeros((NB, 128), jnp.float32)
            else:
                x_ref[b, o:o + NB, 0:128] = row[:, 0:128]
                x_ref[b, o:o + NB, 128:256] = jnp.where(lane64 < base + NB, row[:, 128:256], 0.0)
            if o + NB < N:
                a0 = ((o + NB) // 128) * 128
                rh, rl = halves(row)
                left = jnp.concatenate([rh[:, a0:], rh[:, a0:], rl[:, a0:]], axis=0)
                right = jnp.concatenate([rh, rl, rh], axis=0)
                upd = dot(left, right, TN)[o + NB - a0:, :]
                rest = N - o - NB
                old = x_ref[b, o + NB:, :]
                lane = lax.broadcasted_iota(jnp.int32, (rest, N), 1)
                old = jnp.where((lane >= o) & (lane < o + NB), 0.0, old)
                x_ref[b, o + NB:, :] = old - upd


SCALE = math.sqrt(2 * N)
VMEM = pl.BlockSpec(memory_space=pltpu.VMEM)
SMEM = pl.BlockSpec(memory_space=pltpu.SMEM)


def params(mib):
    return pltpu.CompilerParams(vmem_limit_bytes=mib * 2**20)


def near_kernel(index_ref, count_ref, tiles_ref, source_ref, out_ref):
    row = pl.program_id(0)
    acc = jnp.zeros(out_ref.shape[1:], jnp.float32)
    for k in range(tiles_ref.shape[1]):
        block = source_ref[index_ref[row, k]]
        block = jnp.where(k < count_ref[row], block, jnp.zeros_like(block))
        acc = acc + dot(tiles_ref[0, k], block, NN)
    out_ref[0] = acc


def near_products(tiles, index, counts, source):
    rows, slots, size, _ = tiles.shape
    width = source.shape[2]
    return pl.pallas_call(
        near_kernel,
        grid_spec=pltpu.PrefetchScalarGridSpec(
            num_scalar_prefetch=2,
            grid=(rows,),
            in_specs=[
                pl.BlockSpec((1, slots, size, size), lambda r, *_: (r, 0, 0, 0)),
                pl.BlockSpec(source.shape, lambda r, *_: (0, 0, 0)),
            ],
            out_specs=pl.BlockSpec((1, size, width), lambda r, *_: (r, 0, 0)),
        ),
        out_shape=jax.ShapeDtypeStruct((rows, size, width), jnp.float32),
        compiler_params=params(40),
    )(index, counts, tiles, source)


def gram_kernel(col_ref, own_ref, other_ref, high_ref, low_ref, gram_ref, root_ref):
    first = col_ref[0] == 0
    root = None
    for i in range(own_ref.shape[0]):
        own, other = own_ref[i], other_ref[i]
        full = jnp.concatenate([jnp.where(first, own, other), jnp.where(first, other, own)], axis=1)
        high, low = halves(full)
        high_ref[i] = high
        low_ref[i] = low
        cross = dot(high, low, TN)
        gram = dot(high, high, TN) + (cross + cross.T)
        gram_ref[i] = gram
        root = gram if root is None else root + gram
    root_ref[...] = root


def grams_of(col, own, other):
    leaves, rows, _ = own.shape
    return pl.pallas_call(
        gram_kernel,
        out_shape=[
            jax.ShapeDtypeStruct((leaves, rows, N), jnp.bfloat16),
            jax.ShapeDtypeStruct((leaves, rows, N), jnp.bfloat16),
            jax.ShapeDtypeStruct((leaves, N, N), jnp.float32),
            jax.ShapeDtypeStruct((N, N), jnp.float32),
        ],
        in_specs=[SMEM, VMEM, VMEM],
        out_specs=[VMEM] * 4,
        compiler_params=params(40),
    )(col, own, other)


def apply_inverse(high, low, inverse_rows):
    bh, bl = halves(inverse_rows * SCALE)
    return dot(high, bh, NT) + (dot(high, bl, NT) + dot(low, bh, NT))


def inner_kernel(col_ref, high_ref, low_ref, gram_ref, basis_ref, inner_ref, top_ref, x_ref, m_ref, r_ref):
    leaves = gram_ref.shape[0]
    x_ref[0:leaves] = gram_ref[...]
    at, below = leaves, list(range(leaves))
    merges = []
    while len(below) > 1:
        above = []
        for left, right in zip(below[0::2], below[1::2]):
            x_ref[at] = x_ref[left] + x_ref[right]
            merges.append((at, left, right))
            above.append(at)
            at += 1
        below = above
    factor(x_ref, m_ref, r_ref)
    rows = pl.ds(pl.multiple_of(col_ref[0] * 128, 128), 128)
    for i in range(leaves):
        basis_ref[i] = apply_inverse(high_ref[i], low_ref[i], x_ref[i, rows, :])
    for spot, (parent, left, right) in enumerate(merges):
        for half, child in enumerate((left, right)):
            high, low = halves(r_ref[child])
            inner_ref[spot, N * half:N * half + N, :] = apply_inverse(high, low, x_ref[parent, rows, :])
    top_ref[...] = r_ref[at - 1]


def inner_tree(col, high, low, grams):
    leaves, rows, _ = high.shape
    nodes = 2 * leaves - 1
    return pl.pallas_call(
        inner_kernel,
        out_shape=[
            jax.ShapeDtypeStruct((leaves, rows, 128), jnp.float32),
            jax.ShapeDtypeStruct((leaves - 1, 2 * N, 128), jnp.float32),
            jax.ShapeDtypeStruct((N, N), jnp.float32),
        ],
        in_specs=[SMEM, VMEM, VMEM, VMEM],
        out_specs=[VMEM] * 3,
        scratch_shapes=[
            pltpu.VMEM((nodes, N, N), jnp.float32),
            pltpu.VMEM((nodes, NB, 128), jnp.float32),
            pltpu.VMEM((nodes, N, N), jnp.float32),
        ],
        compiler_params=params(40),
        cost_estimate=pl.CostEstimate(flops=10**10, bytes_accessed=8 * 2**20, transcendentals=0),
    )(col, high, low, grams)


def upper_kernel(col_ref, top_ref, g0, g1, g2, g3, s0, s1, s2, s3, out_ref, x_ref, m_ref, r_ref):
    x_ref[0] = g0[...] + g1[...]
    x_ref[1] = x_ref[0] + (g2[...] + g3[...])
    x_ref[2] = s0[...] + s1[...]
    x_ref[3] = x_ref[2] + (s2[...] + s3[...])
    factor(x_ref, m_ref, r_ref)
    rows = pl.ds(pl.multiple_of(col_ref[0] * 128, 128), 128)
    for level in range(UP):
        high, low = halves(top_ref[...] if level == 0 else r_ref[level - 1])
        out_ref[0, level] = apply_inverse(high, low, x_ref[level, rows, :])


def upper_levels(col, top, near_grams, far_grams):
    return pl.pallas_call(
        upper_kernel,
        out_shape=jax.ShapeDtypeStruct((1, UP, N, 128), jnp.float32),
        in_specs=[SMEM] + [VMEM] * 9,
        out_specs=VMEM,
        scratch_shapes=[
            pltpu.VMEM((UP, N, N), jnp.float32),
            pltpu.VMEM((UP, NB, 128), jnp.float32),
            pltpu.VMEM((UP, N, N), jnp.float32),
        ],
        compiler_params=params(40),
        cost_estimate=pl.CostEstimate(flops=5 * 10**9, bytes_accessed=8 * 2**20, transcendentals=0),
    )(col, top, *near_grams, *far_grams)


def shifted(block, by):
    count = lax.axis_size("leaf")
    return lax.ppermute(block, "leaf", [(i, i + by) for i in range(count) if 0 <= i + by < count])


def mixed(block, mask):
    return lax.ppermute(block, "leaf", [(i, i ^ mask) for i in range(lax.axis_size("leaf"))])


def local(near_tiles, block_cols, row_counts, random_cols):
    blocks_dev, _, tile_size, _ = near_tiles.shape
    col = lax.axis_index("col")[None]
    low, high = shifted(random_cols, 1), shifted(random_cols, -1)
    source = jnp.concatenate([low, random_cols, high], axis=0)
    index = block_cols - (lax.axis_index("leaf") - 1) * blocks_dev
    own = near_products(near_tiles, index, row_counts, source)
    own = own.reshape(blocks_dev // 2, 2 * tile_size, own.shape[2])
    other = lax.ppermute(own, "col", [(0, 1), (1, 0)])
    leaf_high, leaf_low, grams, root = grams_of(col, own, other)
    near_grams = [root] + [mixed(root, mask) for mask in (1, 2, 3)]
    quad = (near_grams[0] + near_grams[1]) + (near_grams[2] + near_grams[3])
    far_grams = [quad] + [mixed(quad, mask) for mask in (4, 8, 12)]
    leaf_basis, inner_transfer, top = inner_tree(col, leaf_high, leaf_low, grams)
    upper_transfer = upper_levels(col, top, near_grams, far_grams)
    return leaf_basis, inner_transfer, upper_transfer


def solution(mesh):
    return jax.shard_map(
        local,
        mesh=mesh,
        in_specs=(P("leaf", None, None, None), P("leaf", None), P("leaf"), P("leaf", None, "col")),
        out_specs=(P("leaf", None, "col"), P("leaf", None, "col"), P("leaf", None, None, "col")),
        check_vma=False,
    )
```

```python
import math

import jax
import jax.numpy as jnp
from jax import lax
from jax.experimental import pallas as pl
from jax.experimental.pallas import tpu as pltpu
from jax.sharding import PartitionSpec as P

N = 256
UP = 4
NB = 64

def stage_shape(batch):
    return (batch, NB, 128)


EVEN = 1


def halves(x):
    high = x.astype(jnp.bfloat16)
    low = (x - high.astype(jnp.float32)).astype(jnp.bfloat16)
    return high, low

def dot(a, b, dims):
    return lax.dot_general(a, b, (dims, ((), ())), preferred_element_type=jnp.float32)

def dot3(a, b, dims):
    ah, al = halves(a)
    bh, bl = halves(b)
    return dot(ah, bh, dims) + (dot(ah, bl, dims) + dot(al, bh, dims))

NN = ((1,), (0,))
NT = ((1,), (1,))
TN = ((0,), (0,))

def factor(x_ref, m_ref, r_ref):
    batch = x_ref.shape[0]
    sub = lax.broadcasted_iota(jnp.int32, (1, 8, 128), 1)
    lane64 = lax.broadcasted_iota(jnp.int32, (NB, 128), 1)
    row64 = lax.broadcasted_iota(jnp.int32, (NB, 128), 0)
    lane8 = lax.broadcasted_iota(jnp.int32, (1, 8, 128), 2)
    full = (batch, 8, 128)
    for p in range(N // NB):
        o = p * NB
        base = o % 128
        other = NB - base
        c0 = o - base
        in_d = (lane64 >= base) & (lane64 < base + NB)
        eye = jnp.where(lane64 - other == row64, 1.0, 0.0).astype(jnp.float32)
        for b in range(batch):
            m_ref[b] = jnp.where(in_d, x_ref[b, o:o + NB, c0:c0 + 128], eye)
        for g in range(NB // 8):
            k0 = base + 8 * g
            top = m_ref[:, 8 * g:8 * g + 8, :]
            cols = [jnp.broadcast_to(top[:, :, k0 + j:k0 + j + 1], full) for j in range(8)]
            t = top
            w = top
            rd_all = jnp.ones(full, jnp.float32)
            trows = []
            for j in range(8):
                rd = jnp.broadcast_to((1.0 / cols[j])[:, j:j + 1, :], full)
                f = jnp.where(sub == j, 0.0, cols[j] * rd)
                trow = jnp.broadcast_to(t[:, j:j + 1, :], full)
                w = jnp.where(sub == j, trow, w)
                rd_all = jnp.where(sub == j, rd, rd_all)
                t = t - f * trow
                for jj in range(j + 1, 8):
                    cols[jj] = cols[jj] - f * jnp.broadcast_to(cols[jj][:, j:j + 1, :], full)
            t = t * rd_all
            w = w * jnp.sqrt(rd_all)
            m_ref[:, 8 * g:8 * g + 8, :] = w
            if g < NB // 8 - 1:
                trows = [jnp.broadcast_to(t[:, j:j + 1, :], full) for j in range(8)]
                for h in range(g + 1, NB // 8):
                    low = m_ref[:, 8 * h:8 * h + 8, :]
                    acc = low
                    for j in range(8):
                        acc = acc - jnp.broadcast_to(low[:, :, k0 + j:k0 + j + 1], full) * trows[j]
                    m_ref[:, 8 * h:8 * h + 8, :] = acc
        for b in range(batch):
            m = m_ref[b]
            inv = m[:, other:other + NB]
            spun = pltpu.roll(m, NB, 1)
            row = dot3(inv, x_ref[b, o:o + NB, :], NN)
            mid = jnp.where(in_d, spun, row[:, c0:c0 + 128])
            row = jnp.concatenate([mid, row[:, 128:]] if c0 == 0 else [row[:, :128], mid], axis=1)
            diag = jnp.where(in_d & (lane64 - base >= row64), m, 0.0)
            if base == 0:
                diag = jnp.where(in_d, diag, row[:, c0:c0 + 128])
            if c0 == 0:
                r_ref[b, o:o + NB, 0:128] = diag
                r_ref[b, o:o + NB, 128:256] = row[:, 128:256]
            else:
                r_ref[b, o:o + NB, 0:128] = jnp.zeros((NB, 128), jnp.float32)
                r_ref[b, o:o + NB, 128:256] = diag
            if c0 == 0:
                keep = jnp.where(lane64 < base + NB, row[:, 0:128], 0.0)
                x_ref[b, o:o + NB, 0:128] = keep
                x_ref[b, o:o + NB, 128:256] = jnp.zeros((NB, 128), jnp.float32)
            else:
                x_ref[b, o:o + NB, 0:128] = row[:, 0:128]
                x_ref[b, o:o + NB, 128:256] = jnp.where(lane64 < base + NB, row[:, 128:256], 0.0)
            if o + NB < N:
                a0 = ((o + NB) // 128) * 128
                rh, rl = halves(row)
                left = jnp.concatenate([rh[:, a0:], rh[:, a0:], rl[:, a0:]], axis=0)
                right = jnp.concatenate([rh, rl, rh], axis=0)
                upd = dot(left, right, TN)[o + NB - a0:, :]
                rest = N - o - NB
                old = x_ref[b, o + NB:, :]
                lane = lax.broadcasted_iota(jnp.int32, (rest, N), 1)
                old = jnp.where((lane >= o) & (lane < o + NB), 0.0, old)
                x_ref[b, o + NB:, :] = old - upd


SCALE = math.sqrt(2 * N)
HALF = N // 2
PACK = 3 * HALF // 2
VMEM = pl.BlockSpec(memory_space=pltpu.VMEM)
SMEM = pl.BlockSpec(memory_space=pltpu.SMEM)
ANY = pl.BlockSpec(memory_space=pl.ANY)


def params(mib):
    return pltpu.CompilerParams(vmem_limit_bytes=mib * 2**20)


def cost(us):
    return pl.CostEstimate(flops=int(us * 10**9), bytes_accessed=2**20, transcendentals=0)


def own_kernel(index_ref, count_ref, tiles_ref, source_ref, out_ref):
    rows, slots = tiles_ref.shape[:2]
    blocks = source_ref.shape[0]

    def one_row(row, carry):
        acc = jnp.zeros(out_ref.shape[1:], jnp.float32)
        for k in range(slots):
            at = index_ref[row, k] - blocks
            live = (k < count_ref[row]) & (at >= 0) & (at < blocks)
            block = source_ref[jnp.clip(at, 0, blocks - 1)]
            acc = acc + dot(tiles_ref[row, k], jnp.where(live, block, jnp.zeros_like(block)), NN)
        out_ref[row] = acc
        return carry

    lax.fori_loop(0, rows, one_row, 0)


def own_products(tiles, index, counts, source):
    rows, _, size, _ = tiles.shape
    return pl.pallas_call(
        own_kernel,
        in_specs=[SMEM, SMEM, VMEM, VMEM],
        out_specs=VMEM,
        out_shape=jax.ShapeDtypeStruct((rows, size, source.shape[2]), jnp.float32),
        compiler_params=params(32),
        cost_estimate=cost(6),
    )(index, counts, tiles, source)


CHUNK = 4


def halo_kernel(index_ref, count_ref, tiles_ref, low_ref, high_ref, part_ref, out_ref, source_ref, list_ref):
    rows, slots = tiles_ref.shape[:2]
    blocks = low_ref.shape[0]
    source_ref[0:blocks] = low_ref[...]
    source_ref[blocks:] = high_ref[...]

    def one_row(row, carry):
        for k in range(slots + 1):
            list_ref[k] = 0
        found = jnp.int32(0)
        for k in range(slots):
            at = index_ref[row, k]
            needed = (k < count_ref[row]) & ((at < blocks) | (at >= 2 * blocks))
            list_ref[found] = k
            found = found + needed.astype(jnp.int32)

        def chunk(first, acc):
            for i in range(first, min(first + CHUNK, slots)):
                k = list_ref[i]
                at = index_ref[row, k]
                at = jnp.clip(jnp.where(at < blocks, at, at - blocks), 0, 2 * blocks - 1)
                block = source_ref[at]
                acc = acc + dot(tiles_ref[row, k], jnp.where(i < found, block, jnp.zeros_like(block)), NN)
            return acc

        out_ref[row] = chunk(0, part_ref[row])
        for first in range(CHUNK, slots, CHUNK):

            @pl.when(found > first)
            def _():
                out_ref[row] = chunk(first, out_ref[row])

        return carry

    lax.fori_loop(0, rows, one_row, 0)


def halo_products(tiles, index, counts, low, high, part):
    rows, slots, _, _ = tiles.shape
    return pl.pallas_call(
        halo_kernel,
        in_specs=[SMEM, SMEM, VMEM, VMEM, VMEM, VMEM],
        out_specs=VMEM,
        out_shape=jax.ShapeDtypeStruct(part.shape, jnp.float32),
        scratch_shapes=[
            pltpu.VMEM((2 * low.shape[0],) + low.shape[1:], low.dtype),
            pltpu.SMEM((slots + 1,), jnp.int32),
        ],
        compiler_params=params(32),
        cost_estimate=cost(3),
    )(index, counts, tiles, low, high, part)


def gram_kernel(col_ref, own_ref, other_ref, high_ref, low_ref, gram_ref, half_ref, pack_ref):
    first = col_ref[0] == 0
    root = None
    for i in range(own_ref.shape[0]):
        own, other = own_ref[i], other_ref[i]
        full = jnp.concatenate([jnp.where(first, own, other), jnp.where(first, other, own)], axis=1)
        high, low = halves(full)
        high_ref[i] = high
        low_ref[i] = low
        cross = dot(high, low, TN)
        gram = dot(high, high, TN) + (cross + cross.T)
        gram_ref[i] = gram
        root = gram if root is None else root + gram
    pack_ref[0:HALF] = root[0:HALF, 0:HALF]
    pack_ref[HALF:2 * HALF] = root[0:HALF, HALF:]
    pack_ref[2 * HALF:] = root[HALF:, HALF:]
    half_ref[...] = pack_ref[pl.ds(pl.multiple_of(col_ref[0] * PACK, 8), PACK), :]


def grams_of(col, own, other):
    leaves, rows, _ = own.shape
    return pl.pallas_call(
        gram_kernel,
        out_shape=[
            jax.ShapeDtypeStruct((leaves, rows, N), jnp.bfloat16),
            jax.ShapeDtypeStruct((leaves, rows, N), jnp.bfloat16),
            jax.ShapeDtypeStruct((leaves, N, N), jnp.float32),
            jax.ShapeDtypeStruct((PACK, HALF), jnp.float32),
        ],
        in_specs=[SMEM, VMEM, VMEM],
        out_specs=[VMEM] * 4,
        scratch_shapes=[pltpu.VMEM((2 * PACK, HALF), jnp.float32)],
        compiler_params=params(32),
        cost_estimate=cost(1),
    )(col, own, other)


def apply_inverse(high, low, inverse_rows):
    bh, bl = halves(inverse_rows * SCALE)
    return dot(high, bh, NT) + (dot(high, bl, NT) + dot(low, bh, NT))


def my_rows(col_ref):
    return pl.ds(pl.multiple_of(col_ref[0] * HALF, HALF), HALF)


def work(batch):
    return [
        pltpu.VMEM((batch, N, N), jnp.float32),
        pltpu.VMEM(stage_shape(batch), jnp.float32),
    ]


def leaf_kernel(col_ref, high_ref, low_ref, gram_ref, basis_ref, r_ref, x_ref, m_ref):
    leaves = gram_ref.shape[0]
    x_ref[...] = gram_ref[...]
    factor(x_ref, m_ref, r_ref)
    rows = my_rows(col_ref)
    for i in range(leaves):
        basis_ref[i] = apply_inverse(high_ref[i], low_ref[i], x_ref[i, rows, :])


def leaf_bases(col, high, low, grams):
    leaves, rows, _ = high.shape
    return pl.pallas_call(
        leaf_kernel,
        out_shape=[
            jax.ShapeDtypeStruct((leaves, rows, HALF), jnp.float32),
            jax.ShapeDtypeStruct((leaves, N, N), jnp.float32),
        ],
        in_specs=[SMEM, VMEM, VMEM, VMEM],
        out_specs=[VMEM] * 2,
        scratch_shapes=work(leaves),
        compiler_params=params(32),
        cost_estimate=cost(14),
    )(col, high, low, grams)


def inner_kernel(col_ref, gram_ref, leaf_r_ref, after_ref, inner_ref, top_ref, x_ref, m_ref, r_ref):
    leaves = gram_ref.shape[0]
    nodes = [("leaf", i) for i in range(leaves)]
    gram_at = {"leaf": gram_ref, "inner": x_ref}
    r_at = {"leaf": leaf_r_ref, "inner": r_ref}
    merges, spot = [], 0
    while len(nodes) > 1:
        above = []
        for left, right in zip(nodes[0::2], nodes[1::2]):
            x_ref[spot] = gram_at[left[0]][left[1]] + gram_at[right[0]][right[1]]
            merges.append((left, right))
            above.append(("inner", spot))
            spot += 1
        nodes = above
    if x_ref.shape[0] > spot:
        x_ref[spot] = x_ref[spot - 1]
    factor(x_ref, m_ref, r_ref)
    rows = my_rows(col_ref)
    for spot, pair in enumerate(merges):
        for half, (kind, child) in enumerate(pair):
            high, low = halves(r_at[kind][child])
            inner_ref[spot, N * half:N * half + N, :] = apply_inverse(high, low, x_ref[spot, rows, :])
    top_ref[...] = r_ref[len(merges) - 1]


def inner_tree(col, grams, leaf_r, after):
    nodes = grams.shape[0] - 1
    batch = nodes + nodes % EVEN
    return pl.pallas_call(
        inner_kernel,
        out_shape=[
            jax.ShapeDtypeStruct((nodes, 2 * N, HALF), jnp.float32),
            jax.ShapeDtypeStruct((N, N), jnp.float32),
        ],
        in_specs=[SMEM, VMEM, VMEM, ANY],
        out_specs=[VMEM] * 2,
        scratch_shapes=work(batch) + [pltpu.VMEM((batch, N, N), jnp.float32)],
        compiler_params=params(32),
        cost_estimate=cost(13),
    )(col, grams, leaf_r, after)


def sum_kernel(own_ref, one_ref, two_ref, three_ref, after_ref, out_ref):
    pair = own_ref[...] + one_ref[...]
    out_ref[0] = pair
    out_ref[1] = pair + (two_ref[...] + three_ref[...])


def level_sums(own, others, after):
    return pl.pallas_call(
        sum_kernel,
        out_shape=jax.ShapeDtypeStruct((2,) + own.shape, jnp.float32),
        in_specs=[VMEM] * 4 + [ANY],
        out_specs=VMEM,
        compiler_params=params(8),
        cost_estimate=cost(0.5),
    )(own, *others, after)


def upper_kernel(col_ref, top_ref, own01, other01, own23, other23, out_ref, x_ref, m_ref, r_ref, pack_ref):
    first = col_ref[0] == 0
    for level in range(UP):
        own, other = ((own01, other01) if level < 2 else (own23, other23))
        mine, theirs = own[level % 2], other[level % 2]
        pack_ref[0:PACK] = jnp.where(first, mine, theirs)
        pack_ref[PACK:] = jnp.where(first, theirs, mine)
        cross = pack_ref[HALF:2 * HALF]
        x_ref[level, 0:HALF, 0:HALF] = pack_ref[0:HALF]
        x_ref[level, 0:HALF, HALF:] = cross
        x_ref[level, HALF:, 0:HALF] = cross.T
        x_ref[level, HALF:, HALF:] = pack_ref[2 * HALF:]
    factor(x_ref, m_ref, r_ref)
    rows = my_rows(col_ref)
    for level in range(UP):
        high, low = halves(top_ref[...] if level == 0 else r_ref[level - 1])
        out_ref[0, level] = apply_inverse(high, low, x_ref[level, rows, :])


def upper_levels(col, top, *sums):
    return pl.pallas_call(
        upper_kernel,
        out_shape=jax.ShapeDtypeStruct((1, UP, N, HALF), jnp.float32),
        in_specs=[SMEM] + [VMEM] * 5,
        out_specs=VMEM,
        scratch_shapes=work(UP)
        + [pltpu.VMEM((UP, N, N), jnp.float32), pltpu.VMEM((2 * PACK, HALF), jnp.float32)],
        compiler_params=params(32),
        cost_estimate=cost(14),
    )(col, top, *sums)


def shifted(block, by):
    count = lax.axis_size("leaf")
    return lax.ppermute(block, "leaf", [(i, i + by) for i in range(count) if 0 <= i + by < count])


def mixed(block, mask):
    return lax.ppermute(block, "leaf", [(i, i ^ mask) for i in range(lax.axis_size("leaf"))])


def swapped(block):
    return lax.ppermute(block, "col", [(0, 1), (1, 0)])


def local(near_tiles, block_cols, row_counts, random_cols):
    blocks_dev, _, tile_size, _ = near_tiles.shape
    col = lax.axis_index("col")[None]
    low, high = shifted(random_cols, 1), shifted(random_cols, -1)
    index = block_cols - (lax.axis_index("leaf") - 1) * blocks_dev
    own = own_products(near_tiles, index, row_counts, random_cols)
    own = halo_products(near_tiles, index, row_counts, low, high, own)
    own = own.reshape(blocks_dev // 2, 2 * tile_size, own.shape[2])
    leaf_high, leaf_low, grams, half = grams_of(col, own, swapped(own))
    near = [mixed(half, mask) for mask in (1, 2, 3)]
    leaf_basis, leaf_r = leaf_bases(col, leaf_high, leaf_low, grams)
    sums01 = level_sums(half, near, leaf_r)
    far = [mixed(sums01[1], mask) for mask in (4, 8, 12)]
    other01 = swapped(sums01)
    inner_transfer, top = inner_tree(col, grams, leaf_r, sums01)
    sums23 = level_sums(sums01[1], far, top)
    other23 = swapped(sums23)
    upper_transfer = upper_levels(col, top, sums01, other01, sums23, other23)
    return leaf_basis, inner_transfer, upper_transfer


def solution(mesh):
    return jax.shard_map(
        local,
        mesh=mesh,
        in_specs=(P("leaf", None, None, None), P("leaf", None), P("leaf"), P("leaf", None, "col")),
        out_specs=(P("leaf", None, "col"), P("leaf", None, "col"), P("leaf", None, None, "col")),
        check_vma=False,
    )
```

```python
import math

import jax
import jax.numpy as jnp
from jax import lax
from jax.experimental import pallas as pl
from jax.experimental.pallas import tpu as pltpu
from jax.sharding import PartitionSpec as P

N = 256
UP = 4
NB = 64

def halves(x):
    high = x.astype(jnp.bfloat16)
    low = (x - high.astype(jnp.float32)).astype(jnp.bfloat16)
    return high, low

def dot(a, b, dims):
    return lax.dot_general(a, b, (dims, ((), ())), preferred_element_type=jnp.float32)

def dot3(a, b, dims):
    ah, al = halves(a)
    bh, bl = halves(b)
    return dot(ah, bh, dims) + (dot(ah, bl, dims) + dot(al, bh, dims))

NN = ((1,), (0,))
NT = ((1,), (1,))
TN = ((0,), (0,))

def stage_shape(batch):
    return (batch // 2, 2, NB, 128)


def tree(terms):
    while len(terms) > 1:
        terms = [a + b for a, b in zip(terms[0::2], terms[1::2])]
    return terms[0]


def spread(x, j):
    return jnp.broadcast_to(x[j:j + 1, :], x.shape)


def split_columns(x, k, second):
    return jnp.take_along_axis(x, jnp.where(second, NB + k, k), axis=1)


def eliminate(m_ref):
    pairs = range(m_ref.shape[0])
    sub = lax.broadcasted_iota(jnp.int32, (8, 128), 0)
    second = lax.broadcasted_iota(jnp.int32, (8, 128), 1) >= NB
    for g in range(NB // 8):
        rows = slice(8 * g, 8 * g + 8)
        td = [m_ref[q, 0, rows, :] for q in pairs]
        ti = [m_ref[q, 1, rows, :] for q in pairs]
        cols = [[split_columns(td[q], 8 * g + j, second) for j in range(8)] for q in pairs]
        wd, wi = list(td), list(ti)
        rd_all = [jnp.ones((8, 128), jnp.float32) for _ in pairs]
        for j in range(8):
            rd = [spread(1.0 / cols[q][j], j) for q in pairs]
            f = [jnp.where(sub == j, 0.0, cols[q][j] * rd[q]) for q in pairs]
            for jj in range(j + 1, 8):
                for q in pairs:
                    cols[q][jj] = cols[q][jj] - f[q] * spread(cols[q][jj], j)
            for q in pairs:
                rowd, rowi = spread(td[q], j), spread(ti[q], j)
                rd_all[q] = jnp.where(sub == j, rd[q], rd_all[q])
                wd[q] = jnp.where(sub == j, rowd, wd[q])
                wi[q] = jnp.where(sub == j, rowi, wi[q])
                td[q] = td[q] - f[q] * rowd
                ti[q] = ti[q] - f[q] * rowi
        for q in pairs:
            root = jnp.sqrt(rd_all[q])
            m_ref[q, 0, rows, :] = wd[q] * root
            m_ref[q, 1, rows, :] = wi[q] * root
            td[q] = td[q] * rd_all[q]
            ti[q] = ti[q] * rd_all[q]
        for h in range(g + 1, NB // 8):
            low = slice(8 * h, 8 * h + 8)
            for q in pairs:
                ld = m_ref[q, 0, low, :]
                factors = [split_columns(ld, 8 * g + j, second) for j in range(8)]
                m_ref[q, 0, low, :] = ld - tree([c * spread(td[q], j) for j, c in enumerate(factors)])
                m_ref[q, 1, low, :] = m_ref[q, 1, low, :] - tree([c * spread(ti[q], j) for j, c in enumerate(factors)])


def factor(x_ref, m_ref, r_ref, panels=range(N // NB), shift=0, valid=None):
    batch = x_ref.shape[0]
    lane = lax.broadcasted_iota(jnp.int32, (NB, 128), 1)
    row_id = lax.broadcasted_iota(jnp.int32, (NB, 128), 0)
    left_half = lane < NB
    eye = jnp.where(lane % NB == row_id, 1.0, 0.0).astype(jnp.float32)
    zero = jnp.zeros((NB, 128), jnp.float32)
    valid = batch if valid is None else valid
    for p in panels:
        o = p * NB
        base = o % 128
        c0 = o - base
        here = slice(o - shift, o - shift + NB)
        below = slice(o - shift + NB, None)

        def placed(x, slot):
            return x if NB * slot == base else pltpu.roll(x, NB, 1)

        in_d = (lane >= base) & (lane < base + NB)
        for q in range(batch // 2):
            d0, d1 = [placed(x_ref[2 * q + s, here, c0:c0 + 128], s) for s in range(2)]
            m_ref[q, 0] = jnp.where(left_half, d0, d1)
            m_ref[q, 1] = eye
        eliminate(m_ref)
        for q in range(batch // 2):
            packed, inverse = m_ref[q, 0], m_ref[q, 1]
            wide = jnp.concatenate([jnp.where(left_half, inverse, 0.0), jnp.where(left_half, 0.0, inverse)], axis=0)
            both = jnp.concatenate([x_ref[2 * q, here, :], x_ref[2 * q + 1, here, :]], axis=0)
            both = dot3(wide, both, NN)
            for s in range(2):
                b = 2 * q + s
                if b >= valid:
                    continue
                row = both[NB * s:NB * s + NB]
                diag = jnp.where(in_d & (lane - base >= row_id), placed(packed, s), 0.0)
                mid = jnp.where(in_d, placed(inverse, s), row[:, c0:c0 + 128])
                if c0 == 0:
                    row = jnp.concatenate([mid, row[:, 128:]], axis=1)
                    r_ref[b, here, 0:128] = jnp.where(in_d, diag, mid) if base == 0 else diag
                    r_ref[b, here, 128:256] = row[:, 128:]
                    x_ref[b, here, 0:128] = jnp.where(lane < base + NB, mid, 0.0)
                    x_ref[b, here, 128:256] = zero
                else:
                    row = jnp.concatenate([row[:, :128], mid], axis=1)
                    r_ref[b, here, 0:128] = zero
                    r_ref[b, here, 128:256] = jnp.where(in_d, diag, mid) if base == 0 else diag
                    x_ref[b, here, 0:128] = row[:, :128]
                    x_ref[b, here, 128:256] = jnp.where(lane < base + NB, mid, 0.0)
                if o + NB < N:
                    a0 = ((o + NB) // 128) * 128
                    rh, rl = halves(row)
                    left = jnp.concatenate([rh[:, a0:], rh[:, a0:], rl[:, a0:]], axis=0)
                    right = jnp.concatenate([rh, rl, rh], axis=0)
                    update = dot(left, right, TN)[o + NB - a0:, :]
                    old = x_ref[b, below, :]
                    at = lax.broadcasted_iota(jnp.int32, old.shape, 1)
                    x_ref[b, below, :] = jnp.where((at >= o) & (at < o + NB), 0.0, old) - update


SCALE = math.sqrt(2 * N)
HALF = N // 2
PACK = 3 * HALF // 2
VMEM = pl.BlockSpec(memory_space=pltpu.VMEM)
SMEM = pl.BlockSpec(memory_space=pltpu.SMEM)
ANY = pl.BlockSpec(memory_space=pl.ANY)


def params(mib):
    return pltpu.CompilerParams(vmem_limit_bytes=mib * 2**20)


def cost(us):
    return pl.CostEstimate(flops=int(us * 10**9), bytes_accessed=2**20, transcendentals=0)


def own_kernel(index_ref, count_ref, tiles_ref, source_ref, out_ref):
    rows, slots = tiles_ref.shape[:2]
    blocks = source_ref.shape[0]

    def one_row(row, carry):
        acc = jnp.zeros(out_ref.shape[1:], jnp.float32)
        for k in range(slots):
            at = index_ref[row, k] - blocks
            live = (k < count_ref[row]) & (at >= 0) & (at < blocks)
            block = source_ref[jnp.clip(at, 0, blocks - 1)]
            acc = acc + dot(tiles_ref[row, k], jnp.where(live, block, jnp.zeros_like(block)), NN)
        out_ref[row] = acc
        return carry

    lax.fori_loop(0, rows, one_row, 0)


def own_products(tiles, index, counts, source):
    rows, _, size, _ = tiles.shape
    return pl.pallas_call(
        own_kernel,
        in_specs=[SMEM, SMEM, VMEM, VMEM],
        out_specs=VMEM,
        out_shape=jax.ShapeDtypeStruct((rows, size, source.shape[2]), jnp.float32),
        compiler_params=params(32),
        cost_estimate=cost(6),
    )(index, counts, tiles, source)


CHUNK = 3


def halo_kernel(index_ref, count_ref, tiles_ref, low_ref, high_ref, part_ref, out_ref, source_ref, list_ref):
    rows, slots = tiles_ref.shape[:2]
    blocks = low_ref.shape[0]
    source_ref[0:blocks] = low_ref[...]
    source_ref[blocks:] = high_ref[...]

    def one_row(row, carry):
        for k in range(slots + 1):
            list_ref[k] = 0
        found = jnp.int32(0)
        for k in range(slots):
            at = index_ref[row, k]
            needed = (k < count_ref[row]) & ((at < blocks) | (at >= 2 * blocks))
            list_ref[found] = k
            found = found + needed.astype(jnp.int32)

        def chunk(first, acc):
            for i in range(first, min(first + CHUNK, slots)):
                k = list_ref[i]
                at = index_ref[row, k]
                at = jnp.clip(jnp.where(at < blocks, at, at - blocks), 0, 2 * blocks - 1)
                block = source_ref[at]
                acc = acc + dot(tiles_ref[row, k], jnp.where(i < found, block, jnp.zeros_like(block)), NN)
            return acc

        out_ref[row] = chunk(0, part_ref[row])
        for first in range(CHUNK, slots, CHUNK):

            @pl.when(found > first)
            def _():
                out_ref[row] = chunk(first, out_ref[row])

        return carry

    lax.fori_loop(0, rows, one_row, 0)


def halo_products(tiles, index, counts, low, high, part):
    rows, slots, _, _ = tiles.shape
    return pl.pallas_call(
        halo_kernel,
        in_specs=[SMEM, SMEM, VMEM, VMEM, VMEM, VMEM],
        out_specs=VMEM,
        out_shape=jax.ShapeDtypeStruct(part.shape, jnp.float32),
        scratch_shapes=[
            pltpu.VMEM((2 * low.shape[0],) + low.shape[1:], low.dtype),
            pltpu.SMEM((slots + 1,), jnp.int32),
        ],
        compiler_params=params(32),
        cost_estimate=cost(3),
    )(index, counts, tiles, low, high, part)


def gram_kernel(col_ref, own_ref, other_ref, high_ref, low_ref, gram_ref, half_ref, pack_ref):
    first = col_ref[0] == 0
    root = None
    for i in range(own_ref.shape[0]):
        own, other = own_ref[i], other_ref[i]
        full = jnp.concatenate([jnp.where(first, own, other), jnp.where(first, other, own)], axis=1)
        high, low = halves(full)
        high_ref[i] = high
        low_ref[i] = low
        cross = dot(high, low, TN)
        gram = dot(high, high, TN) + (cross + cross.T)
        gram_ref[i] = gram
        root = gram if root is None else root + gram
    pack_ref[0:HALF] = root[0:HALF, 0:HALF]
    pack_ref[HALF:2 * HALF] = root[0:HALF, HALF:]
    pack_ref[2 * HALF:] = root[HALF:, HALF:]
    half_ref[...] = pack_ref[pl.ds(pl.multiple_of(col_ref[0] * PACK, 8), PACK), :]


def grams_of(col, own, other):
    leaves, rows, _ = own.shape
    return pl.pallas_call(
        gram_kernel,
        out_shape=[
            jax.ShapeDtypeStruct((leaves, rows, N), jnp.bfloat16),
            jax.ShapeDtypeStruct((leaves, rows, N), jnp.bfloat16),
            jax.ShapeDtypeStruct((leaves, N, N), jnp.float32),
            jax.ShapeDtypeStruct((PACK, HALF), jnp.float32),
        ],
        in_specs=[SMEM, VMEM, VMEM],
        out_specs=[VMEM] * 4,
        scratch_shapes=[pltpu.VMEM((2 * PACK, HALF), jnp.float32)],
        compiler_params=params(32),
        cost_estimate=cost(1),
    )(col, own, other)


def apply_inverse(high, low, inverse_rows):
    bh, bl = halves(inverse_rows * SCALE)
    return dot(high, bh, NT) + (dot(high, bl, NT) + dot(low, bh, NT))


def my_rows(col_ref):
    return pl.ds(pl.multiple_of(col_ref[0] * HALF, HALF), HALF)


def work(batch):
    return [
        pltpu.VMEM((batch, N, N), jnp.float32),
        pltpu.VMEM(stage_shape(batch), jnp.float32),
    ]


def start_kernel(gram_ref, x_ref, r_ref, m_ref):
    leaves = gram_ref.shape[0]
    x_ref[0:leaves] = gram_ref[...]
    nodes, spot = list(range(leaves)), leaves
    while len(nodes) > 1:
        above = []
        for left, right in zip(nodes[0::2], nodes[1::2]):
            x_ref[spot] = x_ref[left] + x_ref[right]
            above.append(spot)
            spot += 1
        nodes = above
    x_ref[spot] = x_ref[spot - 1]
    factor(x_ref, m_ref, r_ref, panels=range(HALF // NB), valid=spot)


def start_factors(grams):
    batch = 2 * grams.shape[0]
    return pl.pallas_call(
        start_kernel,
        out_shape=[jax.ShapeDtypeStruct((batch, N, N), jnp.float32)] * 2,
        in_specs=[VMEM],
        out_specs=[VMEM] * 2,
        scratch_shapes=[pltpu.VMEM(stage_shape(batch), jnp.float32)],
        compiler_params=params(32),
        cost_estimate=cost(11),
    )(grams)


def finish_kernel(
    col_ref, high_ref, low_ref, x_in, r_in, after_ref, basis_ref, inner_ref, top_ref, x_ref, r_ref, m_ref, i_ref
):
    leaves = high_ref.shape[0]
    nodes = 2 * leaves - 1
    x_ref[...] = x_in[:, HALF:, :]
    factor(x_ref, m_ref, r_ref, panels=range(HALF // NB, N // NB), shift=HALF, valid=nodes)
    first = col_ref[0] == 0
    for b in range(nodes):
        i_ref[b] = jnp.where(first, x_in[b, 0:HALF, :], x_ref[b])
    for i in range(leaves):
        basis_ref[i] = apply_inverse(high_ref[i], low_ref[i], i_ref[i])
    for spot in range(leaves - 1):
        for child in (2 * spot, 2 * spot + 1):
            for part, rows in enumerate((r_in[child, 0:HALF, :], r_ref[child])):
                high, low = halves(rows)
                at = N * (child % 2) + HALF * part
                inner_ref[spot, at:at + HALF, :] = apply_inverse(high, low, i_ref[leaves + spot])
    top_ref[0:HALF] = r_in[nodes - 1, 0:HALF, :]
    top_ref[HALF:] = r_ref[nodes - 1]


def finish_tree(col, high, low, x, r, after):
    leaves, rows, _ = high.shape
    batch = x.shape[0]
    half = (batch, HALF, N)
    return pl.pallas_call(
        finish_kernel,
        out_shape=[
            jax.ShapeDtypeStruct((leaves, rows, HALF), jnp.float32),
            jax.ShapeDtypeStruct((leaves - 1, 2 * N, HALF), jnp.float32),
            jax.ShapeDtypeStruct((N, N), jnp.float32),
        ],
        in_specs=[SMEM, VMEM, VMEM, VMEM, VMEM, ANY],
        out_specs=[VMEM] * 3,
        scratch_shapes=[
            pltpu.VMEM(half, jnp.float32),
            pltpu.VMEM(half, jnp.float32),
            pltpu.VMEM(stage_shape(batch), jnp.float32),
            pltpu.VMEM(half, jnp.float32),
        ],
        compiler_params=params(40),
        cost_estimate=cost(12),
    )(col, high, low, x, r, after)


def sum_kernel(own_ref, one_ref, two_ref, three_ref, after_ref, out_ref):
    pair = own_ref[...] + one_ref[...]
    out_ref[0] = pair
    out_ref[1] = pair + (two_ref[...] + three_ref[...])


def level_sums(own, others, after):
    return pl.pallas_call(
        sum_kernel,
        out_shape=jax.ShapeDtypeStruct((2,) + own.shape, jnp.float32),
        in_specs=[VMEM] * 4 + [ANY],
        out_specs=VMEM,
        compiler_params=params(8),
        cost_estimate=cost(0.5),
    )(own, *others, after)


def upper_kernel(col_ref, top_ref, own01, other01, own23, other23, out_ref, x_ref, m_ref, r_ref, pack_ref):
    first = col_ref[0] == 0
    for level in range(UP):
        own, other = ((own01, other01) if level < 2 else (own23, other23))
        mine, theirs = own[level % 2], other[level % 2]
        pack_ref[0:PACK] = jnp.where(first, mine, theirs)
        pack_ref[PACK:] = jnp.where(first, theirs, mine)
        cross = pack_ref[HALF:2 * HALF]
        x_ref[level, 0:HALF, 0:HALF] = pack_ref[0:HALF]
        x_ref[level, 0:HALF, HALF:] = cross
        x_ref[level, HALF:, 0:HALF] = cross.T
        x_ref[level, HALF:, HALF:] = pack_ref[2 * HALF:]
    factor(x_ref, m_ref, r_ref)
    rows = my_rows(col_ref)
    for level in range(UP):
        high, low = halves(top_ref[...] if level == 0 else r_ref[level - 1])
        out_ref[0, level] = apply_inverse(high, low, x_ref[level, rows, :])


def upper_levels(col, top, *sums):
    return pl.pallas_call(
        upper_kernel,
        out_shape=jax.ShapeDtypeStruct((1, UP, N, HALF), jnp.float32),
        in_specs=[SMEM] + [VMEM] * 5,
        out_specs=VMEM,
        scratch_shapes=work(UP)
        + [pltpu.VMEM((UP, N, N), jnp.float32), pltpu.VMEM((2 * PACK, HALF), jnp.float32)],
        compiler_params=params(32),
        cost_estimate=cost(14),
    )(col, top, *sums)


def shifted(block, by):
    count = lax.axis_size("leaf")
    return lax.ppermute(block, "leaf", [(i, i + by) for i in range(count) if 0 <= i + by < count])


def mixed(block, mask):
    return lax.ppermute(block, "leaf", [(i, i ^ mask) for i in range(lax.axis_size("leaf"))])


def swapped(block):
    return lax.ppermute(block, "col", [(0, 1), (1, 0)])


def local(near_tiles, block_cols, row_counts, random_cols):
    blocks_dev, _, tile_size, _ = near_tiles.shape
    col = lax.axis_index("col")[None]
    low, high = shifted(random_cols, 1), shifted(random_cols, -1)
    index = block_cols - (lax.axis_index("leaf") - 1) * blocks_dev
    own = own_products(near_tiles, index, row_counts, random_cols)
    own = halo_products(near_tiles, index, row_counts, low, high, own)
    own = own.reshape(blocks_dev // 2, 2 * tile_size, own.shape[2])
    leaf_high, leaf_low, grams, half = grams_of(col, own, swapped(own))
    near = [mixed(half, mask) for mask in (1, 2, 3)]
    x, r = start_factors(grams)
    sums01 = level_sums(half, near, r)
    far = [mixed(sums01[1], mask) for mask in (4, 8, 12)]
    other01 = swapped(sums01)
    leaf_basis, inner_transfer, top = finish_tree(col, leaf_high, leaf_low, x, r, sums01)
    sums23 = level_sums(sums01[1], far, top)
    other23 = swapped(sums23)
    upper_transfer = upper_levels(col, top, sums01, other01, sums23, other23)
    return leaf_basis, inner_transfer, upper_transfer


def solution(mesh):
    return jax.shard_map(
        local,
        mesh=mesh,
        in_specs=(P("leaf", None, None, None), P("leaf", None), P("leaf"), P("leaf", None, "col")),
        out_specs=(P("leaf", None, "col"), P("leaf", None, "col"), P("leaf", None, None, "col")),
        check_vma=False,
    )
```

```python
import math

import jax
import jax.numpy as jnp
from jax import lax
from jax.experimental import pallas as pl
from jax.experimental.pallas import tpu as pltpu
from jax.sharding import PartitionSpec as P

N = 256
UP = 4
NB = 64

def halves(x):
    high = x.astype(jnp.bfloat16)
    low = (x - high.astype(jnp.float32)).astype(jnp.bfloat16)
    return high, low

def dot(a, b, dims):
    return lax.dot_general(a, b, (dims, ((), ())), preferred_element_type=jnp.float32)

def dot3(a, b, dims):
    ah, al = halves(a)
    bh, bl = halves(b)
    return dot(ah, bh, dims) + (dot(ah, bl, dims) + dot(al, bh, dims))

NN = ((1,), (0,))
NT = ((1,), (1,))
TN = ((0,), (0,))

def stage_shape(batch):
    return (batch // 2, 2, NB, 128)


def tree(terms):
    while len(terms) > 1:
        terms = [a + b for a, b in zip(terms[0::2], terms[1::2])]
    return terms[0]


def spread(x, j):
    return jnp.broadcast_to(x[j:j + 1, :], x.shape)


def split_columns(x, k, second):
    return jnp.take_along_axis(x, jnp.where(second, NB + k, k), axis=1)


def cross_update(m_ref, q):
    top, bottom = slice(0, NB // 2), slice(NB // 2, NB)
    second = lax.broadcasted_iota(jnp.int32, (NB // 2, 128), 1) >= NB
    turned = m_ref[q, 0, top, :].T
    left = jnp.concatenate([turned[NB // 2:NB], turned[3 * NB // 2:]], axis=1)
    right = []
    for part in range(2):
        rows = m_ref[q, part, top, :]
        right.append(jnp.concatenate([jnp.where(second, 0.0, rows), jnp.where(second, rows, 0.0)], axis=0))
    update = dot3(left, jnp.concatenate(right, axis=1), NN)
    for part in range(2):
        m_ref[q, part, bottom, :] = m_ref[q, part, bottom, :] - update[:, 128 * part:128 * part + 128]


def eliminate(m_ref):
    pairs = range(m_ref.shape[0])
    sub = lax.broadcasted_iota(jnp.int32, (8, 128), 0)
    second = lax.broadcasted_iota(jnp.int32, (8, 128), 1) >= NB
    for g in range(NB // 8):
        rows = slice(8 * g, 8 * g + 8)
        td = [m_ref[q, 0, rows, :] for q in pairs]
        ti = [m_ref[q, 1, rows, :] for q in pairs]
        cols = [[split_columns(td[q], 8 * g + j, second) for j in range(8)] for q in pairs]
        wd, wi = list(td), list(ti)
        rd_all = [jnp.ones((8, 128), jnp.float32) for _ in pairs]
        for j in range(8):
            rd = [spread(1.0 / cols[q][j], j) for q in pairs]
            f = [jnp.where(sub == j, 0.0, cols[q][j] * rd[q]) for q in pairs]
            for jj in range(j + 1, 8):
                for q in pairs:
                    cols[q][jj] = cols[q][jj] - f[q] * spread(cols[q][jj], j)
            for q in pairs:
                rowd, rowi = spread(td[q], j), spread(ti[q], j)
                rd_all[q] = jnp.where(sub == j, rd[q], rd_all[q])
                wd[q] = jnp.where(sub == j, rowd, wd[q])
                wi[q] = jnp.where(sub == j, rowi, wi[q])
                td[q] = td[q] - f[q] * rowd
                ti[q] = ti[q] - f[q] * rowi
        for q in pairs:
            root = jnp.sqrt(rd_all[q])
            m_ref[q, 0, rows, :] = wd[q] * root
            m_ref[q, 1, rows, :] = wi[q] * root
            td[q] = td[q] * rd_all[q]
            ti[q] = ti[q] * rd_all[q]
        for h in range(g + 1, NB // 16 if g < NB // 16 else NB // 8):
            low = slice(8 * h, 8 * h + 8)
            for q in pairs:
                ld = m_ref[q, 0, low, :]
                factors = [split_columns(ld, 8 * g + j, second) for j in range(8)]
                m_ref[q, 0, low, :] = ld - tree([c * spread(td[q], j) for j, c in enumerate(factors)])
                m_ref[q, 1, low, :] = m_ref[q, 1, low, :] - tree([c * spread(ti[q], j) for j, c in enumerate(factors)])
        if g == NB // 16 - 1:
            for q in pairs:
                cross_update(m_ref, q)


def factor(x_ref, m_ref, r_ref, panels=range(N // NB), shift=0, valid=None):
    batch = x_ref.shape[0]
    lane = lax.broadcasted_iota(jnp.int32, (NB, 128), 1)
    row_id = lax.broadcasted_iota(jnp.int32, (NB, 128), 0)
    left_half = lane < NB
    eye = jnp.where(lane % NB == row_id, 1.0, 0.0).astype(jnp.float32)
    zero = jnp.zeros((NB, 128), jnp.float32)
    valid = batch if valid is None else valid
    for p in panels:
        o = p * NB
        base = o % 128
        c0 = o - base
        here = slice(o - shift, o - shift + NB)
        below = slice(o - shift + NB, None)

        def placed(x, slot):
            return x if NB * slot == base else pltpu.roll(x, NB, 1)

        in_d = (lane >= base) & (lane < base + NB)
        for q in range(batch // 2):
            d0, d1 = [placed(x_ref[2 * q + s, here, c0:c0 + 128], s) for s in range(2)]
            m_ref[q, 0] = jnp.where(left_half, d0, d1)
            m_ref[q, 1] = eye
        eliminate(m_ref)
        for q in range(batch // 2):
            packed, inverse = m_ref[q, 0], m_ref[q, 1]
            high = inverse.astype(jnp.bfloat16)
            rest = inverse - high.astype(jnp.float32)
            low = pltpu.roll(rest, NB, 1).astype(jnp.bfloat16)
            none = jnp.zeros_like(high)
            for s in range(2):
                b = 2 * q + s
                if b >= valid:
                    continue
                mine = left_half if s == 0 else ~left_half
                xh, xl = halves(x_ref[b, here, :])
                lhs = jnp.concatenate([jnp.where(mine, high, low), jnp.where(mine, high, none)], axis=1)
                row = dot(lhs, jnp.concatenate([xh, xh, xl, xl], axis=0), NN)
                diag = jnp.where(in_d & (lane - base >= row_id), placed(packed, s), 0.0)
                mid = jnp.where(in_d, placed(inverse, s), row[:, c0:c0 + 128])
                if c0 == 0:
                    row = jnp.concatenate([mid, row[:, 128:]], axis=1)
                    r_ref[b, here, 0:128] = jnp.where(in_d, diag, mid) if base == 0 else diag
                    r_ref[b, here, 128:256] = row[:, 128:]
                    x_ref[b, here, 0:128] = jnp.where(lane < base + NB, mid, 0.0)
                    x_ref[b, here, 128:256] = zero
                else:
                    row = jnp.concatenate([row[:, :128], mid], axis=1)
                    r_ref[b, here, 0:128] = zero
                    r_ref[b, here, 128:256] = jnp.where(in_d, diag, mid) if base == 0 else diag
                    x_ref[b, here, 0:128] = row[:, :128]
                    x_ref[b, here, 128:256] = jnp.where(lane < base + NB, mid, 0.0)
                if o + NB < N:
                    a0 = ((o + NB) // 128) * 128
                    rh, rl = halves(row)
                    left = jnp.concatenate([rh[:, a0:], rh[:, a0:], rl[:, a0:]], axis=0)
                    right = jnp.concatenate([rh, rl, rh], axis=0)
                    update = dot(left, right, TN)[o + NB - a0:, :]
                    old = x_ref[b, below, :]
                    at = lax.broadcasted_iota(jnp.int32, old.shape, 1)
                    x_ref[b, below, :] = jnp.where((at >= o) & (at < o + NB), 0.0, old) - update


SCALE = math.sqrt(2 * N)
HALF = N // 2
PACK = 3 * HALF // 2
VMEM = pl.BlockSpec(memory_space=pltpu.VMEM)
SMEM = pl.BlockSpec(memory_space=pltpu.SMEM)
ANY = pl.BlockSpec(memory_space=pl.ANY)


def params(mib):
    return pltpu.CompilerParams(vmem_limit_bytes=mib * 2**20)


def cost(us):
    return pl.CostEstimate(flops=int(us * 10**9), bytes_accessed=2**20, transcendentals=0)


def own_kernel(index_ref, count_ref, tiles_ref, source_ref, out_ref, order_ref, found_ref):
    rows, slots = tiles_ref.shape[:2]
    blocks = source_ref.shape[0]

    def one_row(row, carry):
        acc = jnp.zeros(out_ref.shape[1:], jnp.float32)
        for k in range(slots):
            order_ref[row, k] = 0
        found = jnp.int32(0)
        for k in range(slots):
            at = index_ref[row, k] - blocks
            mine = (at >= 0) & (at < blocks)
            order_ref[row, found] = k
            found = found + ((k < count_ref[row]) & ~mine).astype(jnp.int32)
            block = source_ref[jnp.clip(at, 0, blocks - 1)]
            live = (k < count_ref[row]) & mine
            acc = acc + dot(tiles_ref[row, k], jnp.where(live, block, jnp.zeros_like(block)), NN)
        out_ref[row] = acc
        found_ref[row] = found
        return carry

    lax.fori_loop(0, rows, one_row, 0)


def own_products(tiles, index, counts, source):
    rows, slots, size, _ = tiles.shape
    return pl.pallas_call(
        own_kernel,
        in_specs=[SMEM, SMEM, VMEM, VMEM],
        out_specs=[VMEM, SMEM, SMEM],
        out_shape=[
            jax.ShapeDtypeStruct((rows, size, source.shape[2]), jnp.float32),
            jax.ShapeDtypeStruct((rows, slots), jnp.int32),
            jax.ShapeDtypeStruct((rows,), jnp.int32),
        ],
        compiler_params=params(32),
        cost_estimate=cost(6),
    )(index, counts, tiles, source)


CHUNK = 3


def halo_kernel(index_ref, order_ref, found_ref, tiles_ref, low_ref, high_ref, part_ref, out_ref):
    rows, slots = tiles_ref.shape[:2]
    blocks = low_ref.shape[0]

    def one_row(row, carry):
        found = found_ref[row]

        def chunk(first, acc):
            for i in range(first, min(first + CHUNK, slots)):
                k = order_ref[row, i]
                at = index_ref[row, k]
                low = low_ref[jnp.clip(at, 0, blocks - 1)]
                high = high_ref[jnp.clip(at - 2 * blocks, 0, blocks - 1)]
                block = jnp.where(at < blocks, low, high)
                acc = acc + dot(tiles_ref[row, k], jnp.where(i < found, block, jnp.zeros_like(block)), NN)
            return acc

        out_ref[row] = chunk(0, part_ref[row])
        for first in range(CHUNK, slots, CHUNK):

            @pl.when(found > first)
            def _():
                out_ref[row] = chunk(first, out_ref[row])

        return carry

    lax.fori_loop(0, rows, one_row, 0)


def halo_products(tiles, index, order, found, low, high, part):
    return pl.pallas_call(
        halo_kernel,
        in_specs=[SMEM, SMEM, SMEM, VMEM, VMEM, VMEM, VMEM],
        out_specs=VMEM,
        out_shape=jax.ShapeDtypeStruct(part.shape, jnp.float32),
        compiler_params=params(32),
        cost_estimate=cost(3),
    )(index, order, found, tiles, low, high, part)


def gram_kernel(col_ref, own_ref, other_ref, high_ref, low_ref, gram_ref, half_ref, pack_ref):
    first = col_ref[0] == 0
    root = None
    for i in range(own_ref.shape[0]):
        own, other = own_ref[i], other_ref[i]
        full = jnp.concatenate([jnp.where(first, own, other), jnp.where(first, other, own)], axis=1)
        high, low = halves(full)
        high_ref[i] = high
        low_ref[i] = low
        cross = dot(high, low, TN)
        gram = dot(high, high, TN) + (cross + cross.T)
        gram_ref[i] = gram
        root = gram if root is None else root + gram
    pack_ref[0:HALF] = root[0:HALF, 0:HALF]
    pack_ref[HALF:2 * HALF] = root[0:HALF, HALF:]
    pack_ref[2 * HALF:] = root[HALF:, HALF:]
    half_ref[...] = pack_ref[pl.ds(pl.multiple_of(col_ref[0] * PACK, 8), PACK), :]


def grams_of(col, own, other):
    leaves, rows, _ = own.shape
    return pl.pallas_call(
        gram_kernel,
        out_shape=[
            jax.ShapeDtypeStruct((leaves, rows, N), jnp.bfloat16),
            jax.ShapeDtypeStruct((leaves, rows, N), jnp.bfloat16),
            jax.ShapeDtypeStruct((leaves, N, N), jnp.float32),
            jax.ShapeDtypeStruct((PACK, HALF), jnp.float32),
        ],
        in_specs=[SMEM, VMEM, VMEM],
        out_specs=[VMEM] * 4,
        scratch_shapes=[pltpu.VMEM((2 * PACK, HALF), jnp.float32)],
        compiler_params=params(32),
        cost_estimate=cost(1),
    )(col, own, other)


def apply_inverse(high, low, inverse_rows):
    bh, bl = halves(inverse_rows * SCALE)
    return dot(high, bh, NT) + (dot(high, bl, NT) + dot(low, bh, NT))


def my_rows(col_ref):
    return pl.ds(pl.multiple_of(col_ref[0] * HALF, HALF), HALF)


def work(batch):
    return [
        pltpu.VMEM((batch, N, N), jnp.float32),
        pltpu.VMEM(stage_shape(batch), jnp.float32),
    ]


def start_kernel(gram_ref, x_ref, r_ref, m_ref):
    leaves = gram_ref.shape[0]
    x_ref[0:leaves] = gram_ref[...]
    nodes, spot = list(range(leaves)), leaves
    while len(nodes) > 1:
        above = []
        for left, right in zip(nodes[0::2], nodes[1::2]):
            x_ref[spot] = x_ref[left] + x_ref[right]
            above.append(spot)
            spot += 1
        nodes = above
    x_ref[spot] = x_ref[spot - 1]
    factor(x_ref, m_ref, r_ref, panels=range(HALF // NB), valid=spot)


def start_factors(grams):
    batch = 2 * grams.shape[0]
    return pl.pallas_call(
        start_kernel,
        out_shape=[jax.ShapeDtypeStruct((batch, N, N), jnp.float32)] * 2,
        in_specs=[VMEM],
        out_specs=[VMEM] * 2,
        scratch_shapes=[pltpu.VMEM(stage_shape(batch), jnp.float32)],
        compiler_params=params(32),
        cost_estimate=cost(11),
    )(grams)


def finish_kernel(
    col_ref, high_ref, low_ref, x_in, r_in, after_ref, basis_ref, inner_ref, top_ref, x_ref, r_ref, m_ref, i_ref
):
    leaves = high_ref.shape[0]
    nodes = 2 * leaves - 1
    x_ref[...] = x_in[:, HALF:, :]
    factor(x_ref, m_ref, r_ref, panels=range(HALF // NB, N // NB), shift=HALF, valid=nodes)
    first = col_ref[0] == 0
    for b in range(nodes):
        i_ref[b] = jnp.where(first, x_in[b, 0:HALF, :], x_ref[b])
    for i in range(leaves):
        basis_ref[i] = apply_inverse(high_ref[i], low_ref[i], i_ref[i])
    for spot in range(leaves - 1):
        for child in (2 * spot, 2 * spot + 1):
            for part, rows in enumerate((r_in[child, 0:HALF, :], r_ref[child])):
                high, low = halves(rows)
                at = N * (child % 2) + HALF * part
                inner_ref[spot, at:at + HALF, :] = apply_inverse(high, low, i_ref[leaves + spot])
    top_ref[0:HALF] = r_in[nodes - 1, 0:HALF, :]
    top_ref[HALF:] = r_ref[nodes - 1]


def finish_tree(col, high, low, x, r, after):
    leaves, rows, _ = high.shape
    batch = x.shape[0]
    half = (batch, HALF, N)
    return pl.pallas_call(
        finish_kernel,
        out_shape=[
            jax.ShapeDtypeStruct((leaves, rows, HALF), jnp.float32),
            jax.ShapeDtypeStruct((leaves - 1, 2 * N, HALF), jnp.float32),
            jax.ShapeDtypeStruct((N, N), jnp.float32),
        ],
        in_specs=[SMEM, VMEM, VMEM, VMEM, VMEM, ANY],
        out_specs=[VMEM] * 3,
        scratch_shapes=[
            pltpu.VMEM(half, jnp.float32),
            pltpu.VMEM(half, jnp.float32),
            pltpu.VMEM(stage_shape(batch), jnp.float32),
            pltpu.VMEM(half, jnp.float32),
        ],
        compiler_params=params(40),
        cost_estimate=cost(12),
    )(col, high, low, x, r, after)


def sum_kernel(own_ref, one_ref, two_ref, three_ref, after_ref, out_ref):
    pair = own_ref[...] + one_ref[...]
    out_ref[0] = pair
    out_ref[1] = pair + (two_ref[...] + three_ref[...])


def last_sum_kernel(sums_ref, one_ref, two_ref, three_ref, after_ref, out_ref):
    out_ref[0:2] = sums_ref[...]
    pair = sums_ref[1] + one_ref[...]
    out_ref[2] = pair
    out_ref[3] = pair + (two_ref[...] + three_ref[...])


def level_sums(body, levels, own, others, after):
    return pl.pallas_call(
        body,
        out_shape=jax.ShapeDtypeStruct((levels,) + others[0].shape, jnp.float32),
        in_specs=[VMEM] * 4 + [ANY],
        out_specs=VMEM,
        compiler_params=params(8),
        cost_estimate=cost(0.5),
    )(own, *others, after)


def upper_kernel(col_ref, top_ref, own_ref, other_ref, out_ref, x_ref, m_ref, r_ref, pack_ref):
    first = col_ref[0] == 0
    for level in range(UP):
        mine, theirs = own_ref[level], other_ref[level]
        pack_ref[0:PACK] = jnp.where(first, mine, theirs)
        pack_ref[PACK:] = jnp.where(first, theirs, mine)
        cross = pack_ref[HALF:2 * HALF]
        x_ref[level, 0:HALF, 0:HALF] = pack_ref[0:HALF]
        x_ref[level, 0:HALF, HALF:] = cross
        x_ref[level, HALF:, 0:HALF] = cross.T
        x_ref[level, HALF:, HALF:] = pack_ref[2 * HALF:]
    factor(x_ref, m_ref, r_ref)
    rows = my_rows(col_ref)
    for level in range(UP):
        high, low = halves(top_ref[...] if level == 0 else r_ref[level - 1])
        out_ref[0, level] = apply_inverse(high, low, x_ref[level, rows, :])


def upper_levels(col, top, own, other):
    return pl.pallas_call(
        upper_kernel,
        out_shape=jax.ShapeDtypeStruct((1, UP, N, HALF), jnp.float32),
        in_specs=[SMEM] + [VMEM] * 3,
        out_specs=VMEM,
        scratch_shapes=work(UP)
        + [pltpu.VMEM((UP, N, N), jnp.float32), pltpu.VMEM((2 * PACK, HALF), jnp.float32)],
        compiler_params=params(32),
        cost_estimate=cost(14),
    )(col, top, own, other)


def shifted(block, by):
    count = lax.axis_size("leaf")
    return lax.ppermute(block, "leaf", [(i, i + by) for i in range(count) if 0 <= i + by < count])


def mixed(block, mask):
    return lax.ppermute(block, "leaf", [(i, i ^ mask) for i in range(lax.axis_size("leaf"))])


def swapped(block):
    return lax.ppermute(block, "col", [(0, 1), (1, 0)])


def local(near_tiles, block_cols, row_counts, random_cols):
    blocks_dev, _, tile_size, _ = near_tiles.shape
    col = lax.axis_index("col")[None]
    low, high = shifted(random_cols, 1), shifted(random_cols, -1)
    index = block_cols - (lax.axis_index("leaf") - 1) * blocks_dev
    part, order, found = own_products(near_tiles, index, row_counts, random_cols)
    own = halo_products(near_tiles, index, order, found, low, high, part)
    own = own.reshape(blocks_dev // 2, 2 * tile_size, own.shape[2])
    leaf_high, leaf_low, grams, half = grams_of(col, own, swapped(own))
    near = [mixed(half, mask) for mask in (1, 2, 3)]
    x, r = start_factors(grams)
    sums = level_sums(sum_kernel, 2, half, near, r)
    far = [mixed(sums[1], mask) for mask in (4, 8, 12)]
    leaf_basis, inner_transfer, top = finish_tree(col, leaf_high, leaf_low, x, r, sums)
    sums = level_sums(last_sum_kernel, UP, sums, far, top)
    upper_transfer = upper_levels(col, top, sums, swapped(sums))
    return leaf_basis, inner_transfer, upper_transfer


def solution(mesh):
    return jax.shard_map(
        local,
        mesh=mesh,
        in_specs=(P("leaf", None, None, None), P("leaf", None), P("leaf"), P("leaf", None, "col")),
        out_specs=(P("leaf", None, "col"), P("leaf", None, "col"), P("leaf", None, None, "col")),
        check_vma=False,
    )
```

```python
import math

import jax
import jax.numpy as jnp
from jax import lax
from jax.experimental import pallas as pl
from jax.experimental.pallas import tpu as pltpu
from jax.sharding import PartitionSpec as P

N = 256
UP = 4
NB = 64

def halves(x):
    high = x.astype(jnp.bfloat16)
    low = (x - high.astype(jnp.float32)).astype(jnp.bfloat16)
    return high, low

def dot(a, b, dims):
    return lax.dot_general(a, b, (dims, ((), ())), preferred_element_type=jnp.float32)

def dot3(a, b, dims):
    ah, al = halves(a)
    bh, bl = halves(b)
    return dot(ah, bh, dims) + (dot(ah, bl, dims) + dot(al, bh, dims))

NN = ((1,), (0,))
NT = ((1,), (1,))
TN = ((0,), (0,))

def stage_shape(batch):
    return (batch // 2, 2, NB, 128)


def tree(terms):
    while len(terms) > 1:
        terms = [a + b for a, b in zip(terms[0::2], terms[1::2])]
    return terms[0]


def spread(x, j):
    return jnp.broadcast_to(x[j:j + 1, :], x.shape)


def split_columns(x, k, second):
    return jnp.take_along_axis(x, jnp.where(second, NB + k, k), axis=1)


def cross_update(m_ref, q):
    top, bottom = slice(0, NB // 2), slice(NB // 2, NB)
    second = lax.broadcasted_iota(jnp.int32, (NB // 2, 128), 1) >= NB
    turned = m_ref[q, 0, top, :].T
    left = jnp.concatenate([turned[NB // 2:NB], turned[3 * NB // 2:]], axis=1)
    right = []
    for part in range(2):
        rows = m_ref[q, part, top, :]
        right.append(jnp.concatenate([jnp.where(second, 0.0, rows), jnp.where(second, rows, 0.0)], axis=0))
    update = dot3(left, jnp.concatenate(right, axis=1), NN)
    for part in range(2):
        m_ref[q, part, bottom, :] = m_ref[q, part, bottom, :] - update[:, 128 * part:128 * part + 128]


def eliminate(m_ref):
    pairs = range(m_ref.shape[0])
    sub = lax.broadcasted_iota(jnp.int32, (8, 128), 0)
    second = lax.broadcasted_iota(jnp.int32, (8, 128), 1) >= NB
    for g in range(NB // 8):
        rows = slice(8 * g, 8 * g + 8)
        td = [m_ref[q, 0, rows, :] for q in pairs]
        ti = [m_ref[q, 1, rows, :] for q in pairs]
        cols = [[split_columns(td[q], 8 * g + j, second) for j in range(8)] for q in pairs]
        wd, wi = list(td), list(ti)
        rd_all = [jnp.ones((8, 128), jnp.float32) for _ in pairs]
        for j in range(8):
            rd = [spread(1.0 / cols[q][j], j) for q in pairs]
            f = [jnp.where(sub == j, 0.0, cols[q][j] * rd[q]) for q in pairs]
            for jj in range(j + 1, 8):
                for q in pairs:
                    cols[q][jj] = cols[q][jj] - f[q] * spread(cols[q][jj], j)
            for q in pairs:
                rowd, rowi = spread(td[q], j), spread(ti[q], j)
                rd_all[q] = jnp.where(sub == j, rd[q], rd_all[q])
                wd[q] = jnp.where(sub == j, rowd, wd[q])
                wi[q] = jnp.where(sub == j, rowi, wi[q])
                td[q] = td[q] - f[q] * rowd
                ti[q] = ti[q] - f[q] * rowi
        for q in pairs:
            root = jnp.sqrt(rd_all[q])
            m_ref[q, 0, rows, :] = wd[q] * root
            m_ref[q, 1, rows, :] = wi[q] * root
            td[q] = td[q] * rd_all[q]
            ti[q] = ti[q] * rd_all[q]
        for h in range(g + 1, NB // 16 if g < NB // 16 else NB // 8):
            low = slice(8 * h, 8 * h + 8)
            for q in pairs:
                ld = m_ref[q, 0, low, :]
                factors = [split_columns(ld, 8 * g + j, second) for j in range(8)]
                m_ref[q, 0, low, :] = ld - tree([c * spread(td[q], j) for j, c in enumerate(factors)])
                m_ref[q, 1, low, :] = m_ref[q, 1, low, :] - tree([c * spread(ti[q], j) for j, c in enumerate(factors)])
        if g == NB // 16 - 1:
            for q in pairs:
                cross_update(m_ref, q)


def factor(x_ref, m_ref, r_ref, panels=range(N // NB), shift=0, valid=None):
    batch = x_ref.shape[0]
    lane = lax.broadcasted_iota(jnp.int32, (NB, 128), 1)
    row_id = lax.broadcasted_iota(jnp.int32, (NB, 128), 0)
    left_half = lane < NB
    eye = jnp.where(lane % NB == row_id, 1.0, 0.0).astype(jnp.float32)
    zero = jnp.zeros((NB, 128), jnp.float32)
    valid = batch if valid is None else valid
    for p in panels:
        o = p * NB
        base = o % 128
        c0 = o - base
        here = slice(o - shift, o - shift + NB)
        below = slice(o - shift + NB, None)

        def placed(x, slot):
            return x if NB * slot == base else pltpu.roll(x, NB, 1)

        in_d = (lane >= base) & (lane < base + NB)
        for q in range(batch // 2):
            d0, d1 = [placed(x_ref[2 * q + s, here, c0:c0 + 128], s) for s in range(2)]
            m_ref[q, 0] = jnp.where(left_half, d0, d1)
            m_ref[q, 1] = eye
        eliminate(m_ref)
        for q in range(batch // 2):
            packed, inverse = m_ref[q, 0], m_ref[q, 1]
            high = inverse.astype(jnp.bfloat16)
            rest = inverse - high.astype(jnp.float32)
            low = pltpu.roll(rest, NB, 1).astype(jnp.bfloat16)
            none = jnp.zeros_like(high)
            for s in range(2):
                b = 2 * q + s
                if b >= valid:
                    continue
                mine = left_half if s == 0 else ~left_half
                xh, xl = halves(x_ref[b, here, :])
                lhs = jnp.concatenate([jnp.where(mine, high, low), jnp.where(mine, high, none)], axis=1)
                row = dot(lhs, jnp.concatenate([xh, xh, xl, xl], axis=0), NN)
                diag = jnp.where(in_d & (lane - base >= row_id), placed(packed, s), 0.0)
                mid = jnp.where(in_d, placed(inverse, s), row[:, c0:c0 + 128])
                if c0 == 0:
                    row = jnp.concatenate([mid, row[:, 128:]], axis=1)
                    r_ref[b, here, 0:128] = jnp.where(in_d, diag, mid) if base == 0 else diag
                    r_ref[b, here, 128:256] = row[:, 128:]
                    x_ref[b, here, 0:128] = jnp.where(lane < base + NB, mid, 0.0)
                    x_ref[b, here, 128:256] = zero
                else:
                    row = jnp.concatenate([row[:, :128], mid], axis=1)
                    r_ref[b, here, 0:128] = zero
                    r_ref[b, here, 128:256] = jnp.where(in_d, diag, mid) if base == 0 else diag
                    x_ref[b, here, 0:128] = row[:, :128]
                    x_ref[b, here, 128:256] = jnp.where(lane < base + NB, mid, 0.0)
                if o + NB < N:
                    a0 = ((o + NB) // 128) * 128
                    rh, rl = halves(row)
                    left = jnp.concatenate([rh[:, a0:], rh[:, a0:], rl[:, a0:]], axis=0)
                    right = jnp.concatenate([rh, rl, rh], axis=0)
                    update = dot(left, right, TN)[o + NB - a0:, :]
                    old = x_ref[b, below, :]
                    at = lax.broadcasted_iota(jnp.int32, old.shape, 1)
                    x_ref[b, below, :] = jnp.where((at >= o) & (at < o + NB), 0.0, old) - update


SCALE = math.sqrt(2 * N)
HALF = N // 2
PACK = 3 * HALF // 2
VMEM = pl.BlockSpec(memory_space=pltpu.VMEM)
SMEM = pl.BlockSpec(memory_space=pltpu.SMEM)
ANY = pl.BlockSpec(memory_space=pl.ANY)


def params(mib):
    return pltpu.CompilerParams(vmem_limit_bytes=mib * 2**20)


def cost(us):
    return pl.CostEstimate(flops=int(us * 10**9), bytes_accessed=2**20, transcendentals=0)


def own_kernel(
    index_ref, count_ref, tiles_any, source_ref, out_ref, order_ref, found_ref, tiles_ref, arrived
):
    rows, slots = tiles_ref.shape[:2]
    for row in range(rows):
        pltpu.make_async_copy(tiles_any.at[row], tiles_ref.at[row], arrived.at[row]).start()
    blocks = source_ref.shape[0]

    def one_row(row, carry):
        acc = jnp.zeros(out_ref.shape[1:], jnp.float32)
        for k in range(slots):
            order_ref[row, k] = 0
        found = jnp.int32(0)
        pltpu.make_async_copy(tiles_any.at[row], tiles_ref.at[row], arrived.at[row]).wait()
        for k in range(slots):
            at = index_ref[row, k] - blocks
            mine = (at >= 0) & (at < blocks)
            order_ref[row, found] = k
            found = found + ((k < count_ref[row]) & ~mine).astype(jnp.int32)
            block = source_ref[jnp.clip(at, 0, blocks - 1)]
            live = (k < count_ref[row]) & mine
            acc = acc + dot(tiles_ref[row, k], jnp.where(live, block, jnp.zeros_like(block)), NN)
        out_ref[row] = acc
        found_ref[row] = found
        return carry

    lax.fori_loop(0, rows, one_row, 0)


def own_products(tiles, index, counts, source):
    rows, slots, size, _ = tiles.shape
    return pl.pallas_call(
        own_kernel,
        in_specs=[SMEM, SMEM, ANY, VMEM],
        out_specs=[VMEM, SMEM, SMEM, VMEM],
        out_shape=[
            jax.ShapeDtypeStruct((rows, size, source.shape[2]), jnp.float32),
            jax.ShapeDtypeStruct((rows, slots), jnp.int32),
            jax.ShapeDtypeStruct((rows,), jnp.int32),
            jax.ShapeDtypeStruct(tiles.shape, tiles.dtype),
        ],
        scratch_shapes=[pltpu.SemaphoreType.DMA((rows,))],
        compiler_params=params(38),
        cost_estimate=cost(6),
    )(index, counts, tiles, source)


CHUNK = 3


def halo_kernel(index_ref, order_ref, found_ref, tiles_ref, low_ref, high_ref, part_ref, out_ref):
    rows, slots = tiles_ref.shape[:2]
    blocks = low_ref.shape[0]

    def one_row(row, carry):
        found = found_ref[row]

        def chunk(first, acc):
            for i in range(first, min(first + CHUNK, slots)):
                k = order_ref[row, i]
                at = index_ref[row, k]
                low = low_ref[jnp.clip(at, 0, blocks - 1)]
                high = high_ref[jnp.clip(at - 2 * blocks, 0, blocks - 1)]
                block = jnp.where(at < blocks, low, high)
                acc = acc + dot(tiles_ref[row, k], jnp.where(i < found, block, jnp.zeros_like(block)), NN)
            return acc

        out_ref[row] = chunk(0, part_ref[row])
        for first in range(CHUNK, slots, CHUNK):

            @pl.when(found > first)
            def _():
                out_ref[row] = chunk(first, out_ref[row])

        return carry

    lax.fori_loop(0, rows, one_row, 0)


def halo_products(tiles, index, order, found, low, high, part):
    return pl.pallas_call(
        halo_kernel,
        in_specs=[SMEM, SMEM, SMEM, VMEM, VMEM, VMEM, VMEM],
        out_specs=VMEM,
        out_shape=jax.ShapeDtypeStruct(part.shape, jnp.float32),
        compiler_params=params(32),
        cost_estimate=cost(3),
    )(index, order, found, tiles, low, high, part)


def gram_kernel(col_ref, own_ref, other_ref, high_ref, low_ref, gram_ref, half_ref, pack_ref):
    first = col_ref[0] == 0
    root = None
    for i in range(own_ref.shape[0]):
        own, other = own_ref[i], other_ref[i]
        full = jnp.concatenate([jnp.where(first, own, other), jnp.where(first, other, own)], axis=1)
        high, low = halves(full)
        high_ref[i] = high
        low_ref[i] = low
        cross = dot(high, low, TN)
        gram = dot(high, high, TN) + (cross + cross.T)
        gram_ref[i] = gram
        root = gram if root is None else root + gram
    pack_ref[0:HALF] = root[0:HALF, 0:HALF]
    pack_ref[HALF:2 * HALF] = root[0:HALF, HALF:]
    pack_ref[2 * HALF:] = root[HALF:, HALF:]
    half_ref[...] = pack_ref[pl.ds(pl.multiple_of(col_ref[0] * PACK, 8), PACK), :]


def grams_of(col, own, other):
    leaves, rows, _ = own.shape
    return pl.pallas_call(
        gram_kernel,
        out_shape=[
            jax.ShapeDtypeStruct((leaves, rows, N), jnp.bfloat16),
            jax.ShapeDtypeStruct((leaves, rows, N), jnp.bfloat16),
            jax.ShapeDtypeStruct((leaves, N, N), jnp.float32),
            jax.ShapeDtypeStruct((PACK, HALF), jnp.float32),
        ],
        in_specs=[SMEM, VMEM, VMEM],
        out_specs=[VMEM] * 4,
        scratch_shapes=[pltpu.VMEM((2 * PACK, HALF), jnp.float32)],
        compiler_params=params(32),
        cost_estimate=cost(1),
    )(col, own, other)


def apply_inverse(high, low, inverse_rows):
    bh, bl = halves(inverse_rows * SCALE)
    both = dot(high, jnp.concatenate([bh, bl], axis=0), NT)
    return both[:, 0:HALF] + (both[:, HALF:] + dot(low, bh, NT))


def my_rows(col_ref):
    return pl.ds(pl.multiple_of(col_ref[0] * HALF, HALF), HALF)


def work(batch):
    return [
        pltpu.VMEM((batch, N, N), jnp.float32),
        pltpu.VMEM(stage_shape(batch), jnp.float32),
    ]


def start_kernel(gram_ref, x_ref, r_ref, m_ref):
    leaves = gram_ref.shape[0]
    x_ref[0:leaves] = gram_ref[...]
    nodes, spot = list(range(leaves)), leaves
    while len(nodes) > 1:
        above = []
        for left, right in zip(nodes[0::2], nodes[1::2]):
            x_ref[spot] = x_ref[left] + x_ref[right]
            above.append(spot)
            spot += 1
        nodes = above
    x_ref[spot] = x_ref[spot - 1]
    factor(x_ref, m_ref, r_ref, panels=range(HALF // NB), valid=spot)


def start_factors(grams):
    batch = 2 * grams.shape[0]
    return pl.pallas_call(
        start_kernel,
        out_shape=[jax.ShapeDtypeStruct((batch, N, N), jnp.float32)] * 2,
        in_specs=[VMEM],
        out_specs=[VMEM] * 2,
        scratch_shapes=[pltpu.VMEM(stage_shape(batch), jnp.float32)],
        compiler_params=params(32),
        cost_estimate=cost(11),
    )(grams)


def finish_kernel(
    col_ref, high_ref, low_ref, x_in, r_in, after_ref, basis_ref, inner_ref, top_ref, x_ref, r_ref, m_ref, i_ref
):
    leaves = high_ref.shape[0]
    nodes = 2 * leaves - 1
    x_ref[...] = x_in[:, HALF:, :]
    factor(x_ref, m_ref, r_ref, panels=range(HALF // NB, N // NB), shift=HALF, valid=nodes)
    first = col_ref[0] == 0
    for b in range(nodes):
        i_ref[b] = jnp.where(first, x_in[b, 0:HALF, :], x_ref[b])
    for i in range(leaves):
        basis_ref[i] = apply_inverse(high_ref[i], low_ref[i], i_ref[i])
    for spot in range(leaves - 1):
        for child in (2 * spot, 2 * spot + 1):
            for part, rows in enumerate((r_in[child, 0:HALF, :], r_ref[child])):
                high, low = halves(rows)
                at = N * (child % 2) + HALF * part
                inner_ref[spot, at:at + HALF, :] = apply_inverse(high, low, i_ref[leaves + spot])
    top_ref[0:HALF] = r_in[nodes - 1, 0:HALF, :]
    top_ref[HALF:] = r_ref[nodes - 1]


def finish_tree(col, high, low, x, r, after):
    leaves, rows, _ = high.shape
    batch = x.shape[0]
    half = (batch, HALF, N)
    return pl.pallas_call(
        finish_kernel,
        out_shape=[
            jax.ShapeDtypeStruct((leaves, rows, HALF), jnp.float32),
            jax.ShapeDtypeStruct((leaves - 1, 2 * N, HALF), jnp.float32),
            jax.ShapeDtypeStruct((N, N), jnp.float32),
        ],
        in_specs=[SMEM, VMEM, VMEM, VMEM, VMEM, ANY],
        out_specs=[VMEM] * 3,
        scratch_shapes=[
            pltpu.VMEM(half, jnp.float32),
            pltpu.VMEM(half, jnp.float32),
            pltpu.VMEM(stage_shape(batch), jnp.float32),
            pltpu.VMEM(half, jnp.float32),
        ],
        compiler_params=params(40),
        cost_estimate=cost(12),
    )(col, high, low, x, r, after)


def sum_kernel(own_ref, one_ref, two_ref, three_ref, after_ref, out_ref):
    pair = own_ref[...] + one_ref[...]
    out_ref[0] = pair
    out_ref[1] = pair + (two_ref[...] + three_ref[...])


def last_sum_kernel(sums_ref, one_ref, two_ref, three_ref, after_ref, out_ref):
    out_ref[0:2] = sums_ref[...]
    pair = sums_ref[1] + one_ref[...]
    out_ref[2] = pair
    out_ref[3] = pair + (two_ref[...] + three_ref[...])


def level_sums(body, levels, own, others, after):
    return pl.pallas_call(
        body,
        out_shape=jax.ShapeDtypeStruct((levels,) + others[0].shape, jnp.float32),
        in_specs=[VMEM] * 4 + [ANY],
        out_specs=VMEM,
        compiler_params=params(8),
        cost_estimate=cost(0.5),
    )(own, *others, after)


def upper_kernel(col_ref, top_ref, own_ref, other_ref, out_ref, x_ref, m_ref, r_ref, pack_ref):
    first = col_ref[0] == 0
    for level in range(UP):
        mine, theirs = own_ref[level], other_ref[level]
        pack_ref[0:PACK] = jnp.where(first, mine, theirs)
        pack_ref[PACK:] = jnp.where(first, theirs, mine)
        cross = pack_ref[HALF:2 * HALF]
        x_ref[level, 0:HALF, 0:HALF] = pack_ref[0:HALF]
        x_ref[level, 0:HALF, HALF:] = cross
        x_ref[level, HALF:, 0:HALF] = cross.T
        x_ref[level, HALF:, HALF:] = pack_ref[2 * HALF:]
    factor(x_ref, m_ref, r_ref)
    rows = my_rows(col_ref)
    for level in range(UP):
        high, low = halves(top_ref[...] if level == 0 else r_ref[level - 1])
        out_ref[0, level] = apply_inverse(high, low, x_ref[level, rows, :])


def upper_levels(col, top, own, other):
    return pl.pallas_call(
        upper_kernel,
        out_shape=jax.ShapeDtypeStruct((1, UP, N, HALF), jnp.float32),
        in_specs=[SMEM] + [VMEM] * 3,
        out_specs=VMEM,
        scratch_shapes=work(UP)
        + [pltpu.VMEM((UP, N, N), jnp.float32), pltpu.VMEM((2 * PACK, HALF), jnp.float32)],
        compiler_params=params(32),
        cost_estimate=cost(14),
    )(col, top, own, other)


def shifted(block, by):
    count = lax.axis_size("leaf")
    return lax.ppermute(block, "leaf", [(i, i + by) for i in range(count) if 0 <= i + by < count])


def mixed(block, mask):
    return lax.ppermute(block, "leaf", [(i, i ^ mask) for i in range(lax.axis_size("leaf"))])


def swapped(block):
    return lax.ppermute(block, "col", [(0, 1), (1, 0)])


def local(near_tiles, block_cols, row_counts, random_cols):
    blocks_dev, _, tile_size, _ = near_tiles.shape
    col = lax.axis_index("col")[None]
    low, high = shifted(random_cols, 1), shifted(random_cols, -1)
    index = block_cols - (lax.axis_index("leaf") - 1) * blocks_dev
    part, order, found, tiles = own_products(near_tiles, index, row_counts, random_cols)
    own = halo_products(tiles, index, order, found, low, high, part)
    own = own.reshape(blocks_dev // 2, 2 * tile_size, own.shape[2])
    leaf_high, leaf_low, grams, half = grams_of(col, own, swapped(own))
    near = [mixed(half, mask) for mask in (1, 2, 3)]
    x, r = start_factors(grams)
    sums = level_sums(sum_kernel, 2, half, near, r)
    far = [mixed(sums[1], mask) for mask in (4, 8, 12)]
    leaf_basis, inner_transfer, top = finish_tree(col, leaf_high, leaf_low, x, r, sums)
    sums = level_sums(last_sum_kernel, UP, sums, far, top)
    upper_transfer = upper_levels(col, top, sums, swapped(sums))
    return leaf_basis, inner_transfer, upper_transfer


def solution(mesh):
    return jax.shard_map(
        local,
        mesh=mesh,
        in_specs=(P("leaf", None, None, None), P("leaf", None), P("leaf"), P("leaf", None, "col")),
        out_specs=(P("leaf", None, "col"), P("leaf", None, "col"), P("leaf", None, None, "col")),
        check_vma=False,
    )
```
